32 devices in a mesh: ctx: 8 (over z, y), tp: 4 (over x, core).
Axes of the slice: x: 2, y: 2, z: 4, core: 2. Of those that a mesh axis runs over, the one named last changes fastest.
Arguments:
- residual: bfloat16 [2048, 8192], P('ctx', 'tp'), may hold values from -90 to 90
- hyena_gate: bfloat16 [2048, 8192], P('ctx', 'tp'), may hold values from -6 to 6
- hyena_key: bfloat16 [2048, 8192], P('ctx', 'tp'), may hold values from -6 to 6
- hyena_value: bfloat16 [2048, 8192], P('ctx', 'tp'), may hold values from -6 to 6
- filter_taps: float32 [512, 128], P('tp'), may hold values from -0.45 to 0.45
- norm_gain: float32 [8192], P('tp'), may hold values from 0.5 to 1.5
- att_query: bfloat16 [2048, 8192], P('ctx', 'tp'), may hold values from -180 to 180
- att_key: bfloat16 [2048, 8192], P('ctx', 'tp'), may hold values from -6 to 6
- att_value: bfloat16 [2048, 8192], P('ctx', 'tp'), may hold values from -6 to 6
- doc_lengths: int32 [8], replicated, may hold values from 1 to 768, 2048 in all
Outputs:
- normed: bfloat16 [2048, 8192], P('ctx', 'tp')
- attended: bfloat16 [2048, 8192], P('ctx', 'tp')
The draws below stay inside these ranges and needn't reach their ends.
Inputs may be any that keep to these rules, and one draw needn't show every extreme that they name: `doc_lengths`: the lengths sum to 2048; the longest document has exactly 768 tokens.
All inputs are finite; a program needn't handle non-finite values.
Results may differ from the reference program's by a relative error of at most 0.0075.
Values may be sent and summed in bfloat16 or wider, within the bound.
A program may use at most 128 MiB of HBM per device.

```python
import math
import jax
import jax.numpy as jnp
import numpy as np
from jax import lax

D = 8192
HEADS = 64
HEAD_DIM = 128
TAPS = 128
REACH = 3
TOK_DEV = 256
GROUPS = 512
SEQ = 2048
MAXDOC = 768
NDOCS = 8
N_CTX = 8


def draw_residual(key, part):
    base = jax.random.truncated_normal(key, -6.0, 6.0, (SEQ, D), jnp.float32)
    ramp = 0.5 * jnp.sqrt(1.0 + 8.0 * jnp.arange(D, dtype=jnp.float32) / (D - 1))
    values = base * ramp[None, :]
    return values.astype(jnp.bfloat16)


def attention_pair(key):
    base = jax.random.fold_in(key, 7)
    query_key, keys_key = jax.random.split(base)
    shape = (SEQ, HEADS * HEAD_DIM)
    query = jax.random.truncated_normal(query_key, -6.0, 6.0, shape, jnp.float32)
    keys = jax.random.truncated_normal(keys_key, -6.0, 6.0, shape, jnp.float32)
    return (query, keys)


def draw_att_query(key, part):
    return attention_pair(key)[0].astype(jnp.bfloat16)


def draw_att_key(key, part):
    return attention_pair(key)[1].astype(jnp.bfloat16)


def block_levels(key, shape, cuts, low, largest):
    def one(axis_at, shards_of):
        draws = jax.random.uniform(jax.random.fold_in(jax.random.fold_in(key, 6), axis_at), (shards_of,), jnp.float32, low / len(cuts), largest / len(cuts))
        return jnp.repeat(jnp.exp(draws), shape[axis_at] // shards_of).reshape((-1,) + (1,) * (len(shape) - axis_at - 1))

    level = one(*cuts[0])
    for cut in cuts[1:]:
        level = level * one(*cut)
    return level


def split_up(amount, total, limit, slope):
    weights = [(1 << 20) // math.isqrt(grade ** slope) + 1 for grade in range(2, amount + 1)]
    surplus, given = total - limit - (amount - 1), [1] * (amount - 1)
    while surplus > 0:
        movable = [i for i in range(amount - 1) if given[i] < limit]
        whole, remaining = sum([weights[i] for i in movable]), surplus
        for i in movable:
            more = min(limit - given[i], max(1, remaining * weights[i] // whole), surplus)
            given[i] = given[i] + more
            surplus = surplus - more
    return np.array([limit] + given)


def uneven_parts(stream_key, count, total, most, lean):
    if count == 2:
        one = jax.random.randint(stream_key, (), max(1, total - most), min(most, total - 1) + 1)
        return jnp.stack([one, total - one])
    sizes = jnp.asarray(split_up(count, total, most, lean), jnp.int32)
    twos = (count - 1) // 2
    donor, receiver = sizes[1:1 + 2 * twos:2], sizes[2:2 + 2 * twos:2]
    room = jnp.minimum(donor - 1, most - receiver)
    shifted = jax.random.randint(jax.random.fold_in(stream_key, 1), (twos,), 0, 1 << 20) % (room + 1)
    sizes = sizes.at[1:1 + 2 * twos:2].set(donor - shifted).at[2:2 + 2 * twos:2].set(receiver + shifted)
    return sizes[jax.random.permutation(jax.random.fold_in(stream_key, 2), count)]


def scatter_about(stream_key, dims, deviation, bound, cuts=(), held_as=jnp.bfloat16):
    entries = jax.random.normal(stream_key, dims, jnp.float32) * deviation
    if len(cuts) > 0:
        entries = block_levels(stream_key, dims, cuts, -0.22, 0.18) * entries
    return jnp.clip(entries, min=-bound, max=bound).astype(held_as)


def setup_inputs(seed: int = 0) -> dict:
    streams_of = jax.random.split(jax.random.key(seed), 11)
    residual = draw_residual(jax.random.fold_in(streams_of[10], 71), 0)
    hyena_gate = scatter_about(streams_of[1], (SEQ, D), 1.0, 6.0, ((0, 8), (1, 4)))
    hyena_key = scatter_about(streams_of[2], (SEQ, D), 1.0, 6.0, ((0, 8), (1, 4)))
    hyena_value = scatter_about(streams_of[3], (SEQ, D), 1.0, 6.0, ((0, 8), (1, 4)))
    filter_taps = scatter_about(streams_of[4], (GROUPS, TAPS), 0.09, 0.45, ((0, 4),), jnp.float32)
    norm_gain = jnp.clip(1.0 + 0.1 * jax.random.normal(streams_of[5], (D,), jnp.float32), 0.5, 1.5)
    att_query = draw_att_query(jax.random.fold_in(streams_of[10], 71), 0)
    att_key = draw_att_key(jax.random.fold_in(streams_of[10], 71), 0)
    att_value = scatter_about(streams_of[8], (SEQ, HEADS * HEAD_DIM), 1.0, 6.0, ((0, 8), (1, 4)))
    doc_lengths = uneven_parts(streams_of[9], NDOCS, SEQ, MAXDOC, 2).astype(jnp.int32)
    return {"residual": residual, "hyena_gate": hyena_gate, "hyena_key": hyena_key, "hyena_value": hyena_value, "filter_taps": filter_taps, "norm_gain": norm_gain, "att_query": att_query, "att_key": att_key, "att_value": att_value, "doc_lengths": doc_lengths}


norm_epsilon = 1e-05

def document_begin(doc_lengths, positions):
    starts = jnp.cumsum(doc_lengths).astype(jnp.int32) - doc_lengths
    return lax.optimization_barrier(jnp.max(jnp.where(starts[None, :] <= positions[:, None], starts[None, :], 0), axis=1)).astype(jnp.int32)

def causal_filter(extended, filter_taps, reach_back, out_rows):
    groups, taps = filter_taps.shape
    channels = extended.shape[1]
    width = channels // groups
    lag_table = jnp.arange(taps, dtype=jnp.int32)[:, None] + (taps - 1) - jnp.arange(2 * taps - 1, dtype=jnp.int32)[None, :]
    inside = (lag_table >= 0) & (lag_table < taps)
    clipped = jnp.clip(lag_table, 0, taps - 1)
    toeplitz = jnp.where(inside[None], filter_taps[:, clipped], jnp.float32(0.0))

    def one_block(block_index):
        first = (block_index * taps).astype(jnp.int32)
        sources = lax.dynamic_slice_in_dim(extended, first, 2 * taps - 1, 0).astype(jnp.float32)
        sources = sources.reshape(2 * taps - 1, groups, width)
        limits = lax.dynamic_slice_in_dim(reach_back, first, taps, 0)
        valid = lag_table <= limits[:, None]
        kernel = jnp.where(valid[None], toeplitz, jnp.float32(0.0))
        result = jnp.einsum('gts,sgc->tgc', kernel, sources, precision=lax.Precision.HIGHEST)
        return result.reshape(taps, channels)
    blocks = lax.map(one_block, jnp.arange(out_rows // taps, dtype=jnp.int32))
    return blocks.reshape(out_rows, channels)

def attend_one(query_head, key_head, value_head, visible, scale):
    scores = lax.dot_general(query_head, key_head, (((1,), (1,)), ((), ())), preferred_element_type=jnp.float32) * scale
    scores = jnp.where(visible, scores, jnp.float32(-1e+30))
    top = lax.optimization_barrier(jnp.max(scores, axis=1, keepdims=True))
    expo = jnp.where(visible, jnp.exp(scores - top), jnp.float32(0.0))
    denominator = lax.optimization_barrier(jnp.sum(expo, axis=1, keepdims=True))
    summed = jnp.dot(expo.astype(jnp.bfloat16), value_head, preferred_element_type=jnp.float32)
    return (summed / denominator).astype(jnp.bfloat16)

def reference(residual, hyena_gate, hyena_key, hyena_value, filter_taps, norm_gain, att_query, att_key, att_value, doc_lengths):
    positions = jnp.arange(SEQ, dtype=jnp.int32)
    doc_begin = document_begin(doc_lengths, positions)
    mixed = (hyena_key.astype(jnp.float32) * hyena_value.astype(jnp.float32)).astype(jnp.bfloat16)
    extended = jnp.concatenate([jnp.zeros((TAPS - 1, D), jnp.bfloat16), mixed], axis=0)
    filtered = causal_filter(extended, filter_taps, positions - doc_begin, SEQ)
    hidden = residual.astype(jnp.float32) + hyena_gate.astype(jnp.float32) * filtered
    mean_square = lax.optimization_barrier(jnp.mean(hidden * hidden, axis=1, keepdims=True))
    normed = (hidden * lax.rsqrt(mean_square + norm_epsilon) * norm_gain[None, :]).astype(jnp.bfloat16)
    window = (REACH + 1) * TOK_DEV
    front = jnp.zeros((REACH * TOK_DEV, HEADS * HEAD_DIM), jnp.bfloat16)
    padded_keys = jnp.concatenate([front, att_key], axis=0)
    padded_values = jnp.concatenate([front, att_value], axis=0)
    scale = jnp.float32(1.0 / HEAD_DIM ** 0.5)

    def one_shard(block_index):
        first = (block_index * TOK_DEV).astype(jnp.int32)
        query_rows = lax.dynamic_slice_in_dim(att_query, first, TOK_DEV, 0)
        key_rows = lax.dynamic_slice_in_dim(padded_keys, first, window, 0)
        value_rows = lax.dynamic_slice_in_dim(padded_values, first, window, 0)
        query_pos = first + jnp.arange(TOK_DEV, dtype=jnp.int32)
        key_pos = first - REACH * TOK_DEV + jnp.arange(window, dtype=jnp.int32)
        begin_rows = lax.dynamic_slice_in_dim(doc_begin, first, TOK_DEV, 0)
        visible = (key_pos[None, :] <= query_pos[:, None]) & (key_pos[None, :] >= begin_rows[:, None])
        query_heads = query_rows.reshape(TOK_DEV, HEADS, HEAD_DIM).transpose(1, 0, 2)
        key_heads = key_rows.reshape(window, HEADS, HEAD_DIM).transpose(1, 0, 2)
        value_heads = value_rows.reshape(window, HEADS, HEAD_DIM).transpose(1, 0, 2)
        outputs = lax.map(lambda trio: attend_one(trio[0], trio[1], trio[2], visible, scale), (query_heads, key_heads, value_heads))
        return outputs.transpose(1, 0, 2).reshape(TOK_DEV, HEADS * HEAD_DIM)
    attended = lax.map(one_shard, jnp.arange(N_CTX, dtype=jnp.int32)).reshape(SEQ, HEADS * HEAD_DIM)
    return (normed, attended)
```

```python
import functools

import jax
import jax.numpy as jnp
from jax import lax
from jax.experimental import pallas as pl
from jax.experimental.pallas import tpu as pltpu
from jax.sharding import PartitionSpec as P

HEAD_DIM = 128
REACH = 3
LANES = 128
EPSILON = 1e-05
MESH = pl.DeviceIdType.MESH


def kernel(
    model_width,
    res_ref,
    gate_ref,
    hkey_ref,
    hval_ref,
    base_ref,
    gain_ref,
    query_ref,
    key_ref,
    value_ref,
    docs_ref,
    normed_ref,
    attended_ref,
    pairs,
    extended,
    hidden,
    squares,
    bias,
    keep,
    send_sem,
    recv_sem,
    rim_send,
    rim_recv,
    sum_send,
    sum_recv,
):
    shards = lax.axis_size("ctx")
    splits = lax.axis_size("tp")
    me = lax.axis_index("ctx")
    part = lax.axis_index("tp")
    rows, width = res_ref.shape
    taps = keep.shape[1]
    window = (REACH + 1) * rows
    tiles = width // LANES
    chunk = 2 * HEAD_DIM
    chunks = width // chunk
    even = lax.rem(me, 2) == 0
    odd = lax.rem(me, 2) == 1

    barrier = pltpu.get_barrier_semaphore()
    for step in (-2, -1, 1, 2):
        @pl.when((me + step >= 0) & (me + step < shards))
        def _():
            pl.semaphore_signal(barrier, inc=1, device_id={"ctx": me + step}, device_id_type=MESH)
    for step in range(1, splits):
        pl.semaphore_signal(
            barrier, inc=1, device_id={"tp": lax.rem(part + step, splits)}, device_id_type=MESH
        )

    pairs[0, REACH] = key_ref[...]
    pairs[1, REACH] = value_ref[...]
    extended[taps:, :] = (
        hkey_ref[...].astype(jnp.float32) * hval_ref[...].astype(jnp.float32)
    ).astype(jnp.bfloat16)

    @pl.when(me == 0)
    def _():
        extended[:taps, :] = jnp.zeros((taps, width), jnp.bfloat16)

    for distance in range(1, REACH + 1):
        @pl.when(me < distance)
        def _():
            pairs[0, REACH - distance] = jnp.zeros((rows, width), jnp.bfloat16)
            pairs[1, REACH - distance] = jnp.zeros((rows, width), jnp.bfloat16)

    pl.semaphore_wait(
        barrier, jnp.minimum(me, 2) + jnp.minimum(shards - 1 - me, 2) + splits - 1
    )

    def hop(kind, index, source, target, where):
        columns = pl.ds(pl.multiple_of(index * chunk, chunk), chunk)
        return pltpu.make_async_remote_copy(
            src_ref=pairs.at[:, REACH - source, :, columns],
            dst_ref=pairs.at[:, REACH - target, :, columns],
            send_sem=send_sem.at[kind, index],
            recv_sem=recv_sem.at[target - 1, index],
            device_id={"ctx": where},
            device_id_type=MESH,
        )

    def arrive(distance, index):
        columns = pl.ds(pl.multiple_of(index * chunk, chunk), chunk)
        slot = pairs.at[:, REACH - distance, :, columns]
        pltpu.make_async_copy(slot, slot, recv_sem.at[distance - 1, index]).wait()

    has_next = me + 1 < shards
    has_second = me + 2 < shards
    is_first = lambda c: lax.rem(c, 2) == 0
    is_last = lambda c: lax.rem(c, 2) == 1
    always = lambda c: c >= 0
    even_hops = [
        (even & has_second, is_first, 0, 2, 2),
        (even & has_next, always, 0, 1, 1),
        (even & has_next & (me >= 2), is_first, 2, 3, 1),
        (even & has_second & (me >= 1), always, 1, 3, 2),
    ]
    odd_hops = [
        (odd & has_second, always, 0, 2, 2),
        (odd & (me >= 2), always, 2, 1, -1),
        (odd & has_second, is_last, 1, 3, 2),
        (odd & (me >= 3), is_last, 3, 2, -1),
    ]

    def start(table, kind, index):
        condition, takes, source, target, step = table[kind]

        @pl.when(condition & takes(index))
        def _():
            hop(kind, index, source, target, me + step).start()

    def relay(table, kind, index):
        condition, takes, source, target, step = table[kind]

        @pl.when(condition & takes(index))
        def _():
            hop(kind, index, source, target, me + step).start()

    rim = pltpu.make_async_remote_copy(
        src_ref=extended.at[rows : rows + taps],
        dst_ref=extended.at[0:taps],
        send_sem=rim_send,
        recv_sem=rim_recv,
        device_id={"ctx": me + 1},
        device_id_type=MESH,
    )

    @pl.when(has_next)
    def _():
        rim.start()

    def begin(index, carry):
        start(even_hops, 0, index)
        start(even_hops, 1, index)
        start(odd_hops, 0, index)
        return carry

    lax.fori_loop(0, chunks, begin, 0)

    anchor = me * rows
    place = anchor + lax.broadcasted_iota(jnp.int32, (rows, 1), 0)
    first = jnp.zeros((rows, 1), jnp.int32)
    offset = jnp.int32(0)
    for document in range(docs_ref.shape[0]):
        first = jnp.where(place >= offset, jnp.maximum(first, offset), first)
        offset = offset + docs_ref[document]
    sites = anchor - REACH * rows + lax.broadcasted_iota(jnp.int32, (rows, window), 1)
    bias[...] = jnp.where(
        (sites <= place) & (sites >= first), jnp.float32(0.0), jnp.float32(-1e30)
    )
    for block in range(rows // taps):
        span = slice(block * taps, (block + 1) * taps)
        origin = anchor + (block - 1) * taps
        sources = origin + lax.broadcasted_iota(jnp.int32, (taps, 2 * taps), 1)
        keep[block] = jnp.where(sources >= first[span], 1.0, 0.0).astype(jnp.bfloat16)

    @pl.when(me >= 1)
    def _():
        whole = extended.at[0:taps]
        pltpu.make_async_copy(whole, whole, rim_recv).wait()

    group_width = width // base_ref.shape[0]
    per_tile = LANES // group_width
    owner = lax.broadcasted_iota(jnp.int32, (taps, LANES), 1) // group_width
    squares[0] = jnp.zeros((rows, LANES), jnp.float32)

    def filter_tile(tile):
        columns = pl.ds(pl.multiple_of(tile * LANES, LANES), LANES)
        source = extended[:, columns]
        groups = base_ref[pl.ds(pl.multiple_of(tile * per_tile, per_tile), per_tile), :]
        totals = [jnp.zeros((taps, LANES), jnp.float32) for _ in range(rows // taps)]
        for group in range(per_tile):
            spread = jnp.broadcast_to(groups[group : group + 1, :], (taps, 2 * taps))
            toeplitz = pltpu.roll(spread, 0, 1, stride=1, stride_axis=0)
            upper = toeplitz.astype(jnp.bfloat16)
            lower = (toeplitz - upper.astype(jnp.float32)).astype(jnp.bfloat16)
            for block in range(rows // taps):
                mask = keep[block]
                rhs = source[block * taps : (block + 2) * taps]
                result = jnp.dot(upper * mask, rhs, preferred_element_type=jnp.float32)
                result += jnp.dot(lower * mask, rhs, preferred_element_type=jnp.float32)
                totals[block] = jnp.where(owner == group, result, totals[block])
        for block in range(rows // taps):
            span = slice(block * taps, (block + 1) * taps)
            value = (
                res_ref[span, columns].astype(jnp.float32)
                + gate_ref[span, columns].astype(jnp.float32) * totals[block]
            )
            hidden[span, columns] = value
            squares[0, span, :] += value * value

    def first_phase(index, carry):
        def some(step, inner):
            filter_tile(index * (tiles // chunks) + step)
            return inner

        lax.fori_loop(0, tiles // chunks, some, 0)

        @pl.when((me >= 2) & (odd | (even & is_first(index))))
        def _():
            arrive(2, index)

        relay(odd_hops, 1, index)
        relay(even_hops, 2, index)

        @pl.when(me >= 1)
        def _():
            arrive(1, index)

        relay(odd_hops, 2, index)
        relay(even_hops, 3, index)
        return carry

    lax.fori_loop(0, chunks, first_phase, 0)

    def exchange(step):
        return pltpu.make_async_remote_copy(
            src_ref=squares.at[0],
            dst_ref=squares.at[step],
            send_sem=sum_send.at[step],
            recv_sem=sum_recv.at[step],
            device_id={"tp": lax.rem(part + step, splits)},
            device_id_type=MESH,
        )

    for step in range(1, splits):
        exchange(step).start()
    for step in range(1, splits):
        exchange(step).wait_recv()
    total = squares[0]
    for step in range(1, splits):
        total = total + squares[step]
    mean_square = jnp.sum(total, axis=1, keepdims=True) / model_width
    inverse = lax.rsqrt(mean_square + EPSILON)

    def norm_tile(tile, carry):
        columns = pl.ds(pl.multiple_of(tile * LANES, LANES), LANES)
        normed_ref[:, columns] = (hidden[:, columns] * inverse * gain_ref[:, columns]).astype(
            jnp.bfloat16
        )
        return carry

    lax.fori_loop(0, tiles, norm_tile, 0)

    scale = jnp.float32(1.0 / HEAD_DIM**0.5)

    def attend(head):
        columns = pl.ds(pl.multiple_of(head * HEAD_DIM, HEAD_DIM), HEAD_DIM)
        keys = pairs[0, :, :, columns].reshape(window, HEAD_DIM)
        values = pairs[1, :, :, columns].reshape(window, HEAD_DIM)
        scores = lax.dot_general(
            query_ref[:, columns], keys, (((1,), (1,)), ((), ())),
            preferred_element_type=jnp.float32,
        )
        scores = scores * scale + bias[...]
        top = jnp.max(scores, axis=1, keepdims=True)
        expo = jnp.exp(scores - top)
        denominator = jnp.sum(expo, axis=1, keepdims=True)
        summed = jnp.dot(expo.astype(jnp.bfloat16), values, preferred_element_type=jnp.float32)
        attended_ref[:, columns] = (summed / denominator).astype(jnp.bfloat16)

    def second_phase(index, carry):
        @pl.when(me >= 3)
        def _():
            arrive(3, index)

        relay(odd_hops, 3, index)

        @pl.when(even & (me >= 2) & is_last(index))
        def _():
            arrive(2, index)

        for head in range(chunk // HEAD_DIM):
            attend(index * (chunk // HEAD_DIM) + head)
        return carry

    lax.fori_loop(0, chunks, second_phase, 0)

    def finish(index, carry):
        for table in (even_hops, odd_hops):
            for kind in range(4):
                condition, takes, source, target, step = table[kind]

                @pl.when(condition & takes(index))
                def _():
                    hop(kind, index, source, target, me + step).wait_send()
        return carry

    lax.fori_loop(0, chunks, finish, 0)

    @pl.when(has_next)
    def _():
        rim.wait_send()

    for step in range(1, splits):
        exchange(step).wait_send()


def on_device(
    residual, hyena_gate, hyena_key, hyena_value, filter_taps, norm_gain,
    att_query, att_key, att_value, doc_lengths,
):
    rows, width = residual.shape
    groups, taps = filter_taps.shape
    splits = lax.axis_size("tp")
    chunks = width // (2 * HEAD_DIM)
    base = jnp.concatenate(
        [
            jnp.zeros((groups, 1), jnp.float32),
            filter_taps[:, ::-1],
            jnp.zeros((groups, taps - 1), jnp.float32),
        ],
        axis=1,
    )
    in_vmem = pl.BlockSpec(memory_space=pltpu.VMEM)
    return pl.pallas_call(
        functools.partial(kernel, width * splits),
        out_shape=(
            jax.ShapeDtypeStruct((rows, width), jnp.bfloat16),
            jax.ShapeDtypeStruct((rows, width), jnp.bfloat16),
        ),
        in_specs=[in_vmem] * 9 + [pl.BlockSpec(memory_space=pltpu.SMEM)],
        out_specs=(in_vmem, in_vmem),
        scratch_shapes=[
            pltpu.VMEM((2, REACH + 1, rows, width), jnp.bfloat16),
            pltpu.VMEM((rows + taps, width), jnp.bfloat16),
            pltpu.VMEM((rows, width), jnp.float32),
            pltpu.VMEM((splits, rows, LANES), jnp.float32),
            pltpu.VMEM((rows, (REACH + 1) * rows), jnp.float32),
            pltpu.VMEM((rows // taps, taps, 2 * taps), jnp.bfloat16),
            pltpu.SemaphoreType.DMA((4, chunks)),
            pltpu.SemaphoreType.DMA((REACH, chunks)),
            pltpu.SemaphoreType.DMA,
            pltpu.SemaphoreType.DMA,
            pltpu.SemaphoreType.DMA((splits,)),
            pltpu.SemaphoreType.DMA((splits,)),
        ],
        compiler_params=pltpu.CompilerParams(
            collective_id=0, has_side_effects=True, vmem_limit_bytes=50 * 1024 * 1024
        ),
    )(
        residual, hyena_gate, hyena_key, hyena_value, base, norm_gain[None, :],
        att_query, att_key, att_value, doc_lengths,
    )


def solution(mesh):
    both = P("ctx", "tp")
    return jax.shard_map(
        on_device,
        mesh=mesh,
        in_specs=(both, both, both, both, P("tp", None), P("tp"), both, both, both, P()),
        out_specs=(both, both),
        check_vma=False,
    )
```
